512 devices in a mesh: seq: 64 (over z_hi, y, x, core), head: 8 (over z_lo).
Axes of the slice: x: 4, y: 4, z: 16 (z_hi: 2, z_lo: 8; z = z_hi * 8 + z_lo), core: 2. Of those that a mesh axis runs over, the one named last changes fastest.
Arguments:
- clean_query: bfloat16 [512, 5120], P('seq', 'head'), may hold values from -80 to 80
- noise: bfloat16 [512, 5120], P('seq', 'head'), may hold values from -4 to 4
- key_cache: bfloat16 [131072, 1024], P('seq', 'head'), may hold values from -10.5 to 10.5
- value_cache: bfloat16 [131072, 1024], P('seq', 'head'), may hold values from -10 to 10
- out_weight: bfloat16 [5120, 5120], P('head', 'seq'), may hold values from -0.078125 to 0.078125
- row_run: int32 [512], replicated, may hold values from 0 to 15, as said below
- limits: int32 [512], replicated, may hold values from 65 to 131072, as said below
- restored: int32 [16], replicated, may hold values from 64 to 131071, as said below
Outputs:
- traced: bfloat16 [512, 5120], P('head', 'seq')
The draws below stay inside these ranges and needn't reach their ends.
Inputs may be any that keep to these rules, and one draw needn't show every extreme that they name: `row_run`: each run owns exactly 32 rows, in any order. The rows of one run have the limits s + 1 to s + 32 for a start s of that run. restored[r] is limits[i] - 1 of one row i of run r.
All inputs are finite; a program needn't handle non-finite values.
Results may differ from the reference program's by a relative error of at most 0.019.
Values may be sent and summed in bfloat16 or wider, within the bound.
A program may use at most 192 MiB of HBM per device.

```python
import math
import jax
import jax.numpy as jnp
from jax import lax

D = 5120
QH = 40
KV = 8
HD = 128
SUFFIX = 32
RUNS = 16
ROWS = 512
CACHE = 131072


def base_keys(key):
    base_key = jax.random.fold_in(key, 201)
    gaussian = jnp.clip(jax.random.normal(base_key, (CACHE, KV * HD), jnp.float32), -6.0, 6.0)
    return 1.7 * gaussian


def tracing_layout(key):
    shuffled = jax.random.permutation(jax.random.fold_in(key, 101), ROWS).astype(jnp.int32)
    run_of = shuffled // SUFFIX
    slot_index = shuffled % SUFFIX
    coarse = jax.random.randint(jax.random.fold_in(key, 102), (RUNS,), 0, 4096, jnp.int32)
    spread = coarse * coarse // 4096
    start_span = CACHE - 3 * SUFFIX
    run_index = jnp.arange(RUNS, dtype=jnp.int32)
    run_start = 2 * SUFFIX + spread * start_span // 4096
    run_start = jnp.where(run_index == 0, CACHE - SUFFIX, jnp.where(run_index == 1, 2 * SUFFIX, run_start))
    pick_slot = jax.random.randint(jax.random.fold_in(key, 103), (RUNS,), 0, SUFFIX, jnp.int32)
    pick_slot = jnp.where(run_index == 0, SUFFIX - 1, pick_slot)
    restored = (run_start + pick_slot).astype(jnp.int32)
    limits = (run_start[run_of] + slot_index + 1).astype(jnp.int32)
    return (run_of.astype(jnp.int32), limits, restored)


def draw_row_run(key, part):
    layout = tracing_layout(key)
    return layout[0]


def draw_limits(key, part):
    layout = tracing_layout(key)
    return layout[1]


def draw_restored(key, part):
    layout = tracing_layout(key)
    return layout[2]


def draw_key_cache(key, part):
    key_rows = base_keys(key)
    return key_rows.astype(jnp.bfloat16)


def draw_clean_query(key, part):
    key = jax.random.fold_in(key, 11)
    result = 1.7 * jnp.clip(jax.random.normal(key, (ROWS, QH * HD), jnp.float32), -6.0, 6.0)
    return result.astype(jnp.bfloat16)


def block_levels(stream_key, dims, pieces, low, largest):
    level = 1.0
    for dim, shards_of in pieces:
        heights = jax.random.uniform(jax.random.fold_in(jax.random.fold_in(stream_key, 6), dim), (shards_of,), jnp.float32, low / len(pieces), largest / len(pieces))
        level = level * jnp.repeat(jnp.exp(heights), dims[dim] // shards_of).reshape((-1,) + (1,) * (len(dims) - 1 - dim))
    return level


def centred(own_key, shape, width, bound, shards=(), held_as=jnp.bfloat16):
    array = width * jax.random.normal(own_key, shape, jnp.float32)
    if shards:
        array = array * block_levels(own_key, shape, shards, -0.22, 0.18)
    return jnp.clip(array, -bound, bound).astype(held_as)


def setup_inputs(seed: int = 0) -> dict:
    splits = jax.random.split(jax.random.key(seed), 9)
    clean_query = draw_clean_query(jax.random.fold_in(splits[8], 71), 0)
    noise = centred(splits[1], (ROWS, QH * HD), 0.6, 4.0, ((0, 64), (1, 8)))
    key_cache = draw_key_cache(jax.random.fold_in(splits[8], 71), 0)
    value_cache = centred(splits[3], (CACHE, KV * HD), 2.0, 10.0, ((0, 64), (1, 8)))
    out_weight = centred(splits[4], (QH * HD, D), (QH * HD) ** -0.5, 0.078125, ((0, 8), (1, 64)))
    row_run = draw_row_run(jax.random.fold_in(splits[8], 71), 0)
    limits = draw_limits(jax.random.fold_in(splits[8], 71), 0)
    restored = draw_restored(jax.random.fold_in(splits[8], 71), 0)
    return dict(clean_query=clean_query, noise=noise, key_cache=key_cache, value_cache=value_cache, out_weight=out_weight, row_run=row_run, limits=limits, restored=restored)


def corrupt_queries(clean_query, noise, row_run, limits, restored):
    run_table = row_run[:, None] == jnp.arange(RUNS, dtype=jnp.int32)[None, :]
    restored_row = lax.optimization_barrier(jnp.sum(jnp.where(run_table, restored[None, :], 0), axis=1))
    keep_noise = jnp.where(limits - 1 == restored_row, 0.0, 1.0).astype(jnp.float32)
    mixed = clean_query.astype(jnp.float32) + noise.astype(jnp.float32) * keep_noise[:, None]
    return mixed.astype(jnp.bfloat16)

def reference(clean_query, noise, key_cache, value_cache, out_weight, row_run, limits, restored):
    queries = corrupt_queries(clean_query, noise, row_run, limits, restored)
    group_size = QH // KV
    block_rows = math.gcd(ROWS, 64)
    score_scale = 1.0 / math.sqrt(HD)
    position = jnp.arange(CACHE, dtype=jnp.int32)

    def one_head(head_index):
        column = (head_index * HD).astype(jnp.int32)
        key_rows = lax.dynamic_slice_in_dim(key_cache, column, HD, 1).astype(jnp.float32)
        value_rows = lax.dynamic_slice_in_dim(value_cache, column, HD, 1).astype(jnp.float32)
        query_column = (head_index * group_size * HD).astype(jnp.int32)
        head_queries = lax.dynamic_slice_in_dim(queries, query_column, group_size * HD, 1)

        def one_block(block_index):
            first_row = (block_index * block_rows).astype(jnp.int32)
            block_queries = lax.dynamic_slice_in_dim(head_queries, first_row, block_rows, 0)
            block_queries = block_queries.reshape(block_rows, group_size, HD).astype(jnp.float32)
            block_limits = lax.dynamic_slice_in_dim(limits, first_row, block_rows, 0)
            scores = jnp.einsum('bgd,cd->bgc', block_queries, key_rows) * score_scale
            allowed = position[None, None, :] < block_limits[:, None, None]
            row_top = lax.optimization_barrier(jnp.max(jnp.where(allowed, scores, -jnp.inf), axis=2))
            exps = jnp.where(allowed, jnp.exp(scores - row_top[:, :, None]), 0.0)
            row_total = lax.optimization_barrier(jnp.sum(exps, axis=2))
            soft_weights = lax.optimization_barrier(exps.astype(jnp.bfloat16)).astype(jnp.float32)
            weighted = jnp.einsum('bgc,cd->bgd', soft_weights, value_rows)
            normed = weighted / row_total[:, :, None]
            return normed.reshape(block_rows, group_size * HD).astype(jnp.bfloat16)
        blocks_out = lax.map(one_block, jnp.arange(ROWS // block_rows, dtype=jnp.int32))
        return blocks_out.reshape(ROWS, group_size * HD)
    per_head = lax.map(one_head, jnp.arange(KV, dtype=jnp.int32))
    attended = jnp.transpose(per_head, (1, 0, 2)).reshape(ROWS, QH * HD)
    return jnp.dot(attended, out_weight, preferred_element_type=jnp.float32).astype(jnp.bfloat16)
```

```python
import functools
import math

import jax
import jax.numpy as jnp
from jax import lax
from jax.experimental import pallas as pl
from jax.experimental.pallas import tpu as pltpu
from jax.sharding import PartitionSpec as P

MESH = pl.DeviceIdType.MESH
F32 = jnp.float32
BF16 = jnp.bfloat16

HD = 128
GROUP = 5
SCALE = math.log2(math.e) / math.sqrt(HD)
MASKED = -1e30
BLOCK = 16 * GROUP
PACK = BLOCK + 16
CHUNK = 4 * BLOCK
SUB = CHUNK // 2


def lanes_of(shape):
    return lax.broadcasted_iota(jnp.int32, shape, len(shape) - 1)


def pack_stat(rows):
    lane = lanes_of((16, 128))
    tile = jnp.zeros((16, 128), F32)
    for j, row in enumerate(rows):
        tile = jnp.where((lane % 8 == j) & (lane < 24), row, tile)
    high = tile.astype(BF16).astype(F32)
    rest = tile - high
    middle = rest.astype(BF16).astype(F32)
    low = rest - middle
    return jnp.where(lane < 8, high, jnp.where(lane < 16, middle, low)).astype(BF16)


def unpack_stat(tile):
    tile = tile.astype(F32)
    return tile + pltpu.roll(tile, 120, 1) + pltpu.roll(tile, 112, 1)


def head_column(tile, j):
    return jnp.broadcast_to(tile[:, j : j + 1], (16, 128))


def kernel(
    cq_ref, nz_ref, k_hbm, v_hbm, w_hbm, run_ref, lim_ref, restored_ref,
    out_ref,
    k_in, v_in, w_in, own_q, queries, rhs, v_ones, lhs, scores, probs, tops,
    partial, landed, zh_out, zh_in, attended, weights, proj_out, proj_in, limit_col, keep_col,
    load_sem, sib_sem, w_sem, zq_sem, q_send, q_recv, part_send, part_recv, zh_sem, att_send, att_recv, proj_send, proj_recv,
):
    seq, head = lax.axis_index("seq"), lax.axis_index("head")
    shard_len = k_hbm.shape[0]
    cols = w_hbm.shape[1]
    zh, chip, core = seq // 32, (seq // 2) % 16, seq % 2
    y, x = chip // 4, chip % 4

    def device(zh_, chip_, core_, head_):
        return (zh_ * 32 + chip_ * 2 + core_, head_)

    def plane_chip(i):
        return ((y + i // 4) % 4) * 4 + (x + i % 4) % 4

    sibling = device(zh, chip, 1 - core, head)
    zh_peer = device(1 - zh, chip, core, head)

    def remote(src, dst, send, recv, to):
        return pltpu.make_async_remote_copy(
            src_ref=src, dst_ref=dst, send_sem=send, recv_sem=recv, device_id=to, device_id_type=MESH
        )

    barrier = pltpu.get_barrier_semaphore()

    def greet(to):
        pl.semaphore_signal(barrier, inc=1, device_id=to, device_id_type=MESH)

    greet(zh_peer)

    def greet_head(i, _):
        greet(device(zh, chip, (core + i) % 2, (head + i // 2) % 8))
        return 0

    lax.fori_loop(2, 16, greet_head, 0)

    def greet_plane(i, _):
        greet(device(zh, plane_chip(i // 2), (core + i) % 2, head))
        return 0

    lax.fori_loop(1, 32, greet_plane, 0)

    loads = [
        pltpu.make_async_copy(src, dst, load_sem.at[i])
        for i, (src, dst) in enumerate(((k_hbm, k_in), (v_hbm, v_in), (w_hbm, w_in)))
    ]
    for load in loads:
        load.start()

    limits = lim_ref[...]
    runs = run_ref[...]
    restored = jnp.zeros(runs.shape, jnp.int32)
    for r in range(restored_ref.shape[0]):
        restored = jnp.where(runs == r, restored_ref[r], restored)
    keep = jnp.where(limits - 1 == restored, 0.0, 1.0).astype(F32)
    limits = limits.astype(F32)
    diagonal = lax.broadcasted_iota(jnp.int32, (128, 128), 0) == lanes_of((128, 128))
    for t in range(limits.shape[0]):
        for table, column in ((limits, limit_col), (keep, keep_col)):
            spread = jnp.where(diagonal, jnp.broadcast_to(table[t : t + 1, :], (128, 128)), 0.0)
            column[t * 128 : (t + 1) * 128, :] = jnp.broadcast_to(
                jnp.sum(spread, axis=1, keepdims=True), (128, 128)
            )
    my_keep = keep_col[pl.ds(pl.multiple_of(seq * 8, 8), 8), :]
    half_rows = pl.ds(pl.multiple_of(core * 8, 8), 8)
    for j in range(GROUP):
        at = slice(j * HD, (j + 1) * HD)
        own_q[j, half_rows, :] = cq_ref[:, at].astype(F32) + nz_ref[:, at].astype(F32) * my_keep

    row = lax.broadcasted_iota(jnp.int32, (CHUNK, 128), 0)
    one_hot = ((row // BLOCK) * 16 + row % 16) == lanes_of((CHUNK, 128))
    lhs[:, HD:] = jnp.where(one_hot, 1.0, 0.0).astype(BF16)
    rhs[HD + 64 :, :] = jnp.zeros((64, shard_len), BF16)
    v_ones[:, HD:] = jnp.ones((shard_len, HD), BF16)
    loads[0].wait()
    rhs[:HD, :] = k_in[...].T
    loads[1].wait()
    v_ones[:, :HD] = v_in[...]
    loads[2].wait()
    weights[core] = jnp.zeros(weights.shape[1:], BF16)
    weights[core, :, :cols] = w_in[...]

    pl.semaphore_wait(barrier, 46)

    sib_copy = remote(own_q.at[:, half_rows, :], own_q.at[:, half_rows, :], sib_sem.at[0], sib_sem.at[1], sibling)
    sib_copy.start()
    w_copy = remote(weights.at[core], weights.at[core], w_sem.at[0], w_sem.at[1], sibling)
    w_copy.start()
    other_rows = pl.ds(pl.multiple_of(8 - core * 8, 8), 8)
    remote(own_q.at[:, other_rows, :], own_q.at[:, other_rows, :], sib_sem.at[0], sib_sem.at[1], sibling).wait_recv()
    queries[0, chip] = own_q[...].reshape(BLOCK, HD).astype(BF16)
    zq_copy = remote(queries.at[0, chip], queries.at[1, chip], zq_sem.at[0], zq_sem.at[1], zh_peer)
    zq_copy.start()

    def send_queries(rel):
        def step(i, _):
            remote(
                queries.at[rel, chip], queries.at[rel, chip], q_send.at[rel, i], q_recv.at[rel, chip],
                device(zh, plane_chip(i), core, head),
            ).start()
            return 0

        lax.fori_loop(1, 16, step, 0)

    send_queries(0)

    start = (seq * shard_len).astype(F32)

    def chunk(g, _):
        rel, t = g // 4, g % 4
        row_y = (y + t + t // 2 - 2 * (t // 3)) % 4
        zh_of = (zh + rel) % 2

        def arrive(i, _):
            source = row_y * 4 + i

            @pl.when(source != chip)
            def _():
                remote(
                    queries.at[rel, source], queries.at[rel, source], q_send.at[rel, 0], q_recv.at[rel, source], sibling
                ).wait_recv()

            return 0

        lax.fori_loop(0, 4, arrive, 0)
        lhs[:, :HD] = queries[rel, pl.ds(row_y * 4, 4)].reshape(CHUNK, HD)
        first = pl.multiple_of(zh_of * 256 + row_y * 64, 64)
        limit = limit_col[pl.ds(first, 64), :] - start
        for at in range(0, shard_len, 128):
            position = (lanes_of((64, 128)) + at).astype(F32)
            rhs[HD : HD + 64, at : at + 128] = jnp.where(position < limit, 0.0, MASKED).astype(BF16)
        for i in range(4):
            if i < 2:
                scores[i] = jnp.dot(lhs[i * SUB : (i + 1) * SUB, :], rhs[...], preferred_element_type=F32)
            if 1 <= i < 3:
                part = scores[i - 1]
                top = jnp.max(part, axis=1, keepdims=True)
                tops[i - 1] = jnp.broadcast_to(top, (SUB, 128))
                probs[i - 1] = jnp.exp2((part - top) * SCALE).astype(BF16)
            if 2 <= i:
                both = jnp.dot(probs[i - 2], v_ones[...], preferred_element_type=F32)
                total = both[:, HD:]
                mean = (both[:, :HD] / total).astype(BF16)
                stat = tops[i - 2] * SCALE + jnp.log2(total)
                for b in range(2):
                    slot = row_y * 4 + (i - 2) * 2 + b
                    partial[rel, slot, :BLOCK, :] = mean[b * BLOCK : (b + 1) * BLOCK]
                    partial[rel, slot, BLOCK:, :] = pack_stat(
                        [stat[b * BLOCK + j * 16 : b * BLOCK + (j + 1) * 16] for j in range(GROUP)]
                    )

        def depart(i, _):
            owner = row_y * 4 + i
            mine = (owner == chip) & (zh_of == core)

            @pl.when(mine)
            def _():
                landed[seq % 32] = partial[rel, owner]

            @pl.when(jnp.logical_not(mine))
            def _():
                remote(
                    partial.at[rel, owner], landed.at[seq % 32], part_send.at[rel, owner], part_recv.at[seq % 32],
                    device(zh, owner, zh_of, head),
                ).start()

            return 0

        lax.fori_loop(0, 4, depart, 0)
        return 0

    lax.fori_loop(0, 3, chunk, 0)
    zq_copy.wait()
    lax.fori_loop(3, 4, chunk, 0)
    lax.fori_loop(0, 1, lambda i, c: c, 0)
    send_queries(1)
    lax.fori_loop(4, 8, chunk, 0)

    def gather_stat(i, top):
        @pl.when(i != seq % 32)
        def _():
            remote(landed.at[i], landed.at[i], part_send.at[0, 0], part_recv.at[i], sibling).wait_recv()

        return jnp.maximum(top, unpack_stat(landed[i, BLOCK:, :]))

    top = lax.fori_loop(0, 32, gather_stat, jnp.full((16, 128), 2 * MASKED, F32))

    def gather_mean(i, carry):
        total, sums = carry
        weight = jnp.exp2(unpack_stat(landed[i, BLOCK:, :]) - top)
        return total + weight, tuple(
            sums[j] + head_column(weight, j) * landed[i, j * 16 : (j + 1) * 16, :].astype(F32) for j in range(GROUP)
        )

    zero = jnp.zeros((16, 128), F32)
    total, sums = lax.fori_loop(0, 32, gather_mean, (zero, (zero,) * GROUP))
    stat = top + jnp.log2(total)
    means = [sums[j] / head_column(total, j) for j in range(GROUP)]
    for j in range(GROUP):
        zh_out[j * 16 : (j + 1) * 16, :] = means[j].astype(BF16)
    zh_out[BLOCK:, :] = pack_stat([head_column(stat, j) for j in range(GROUP)])
    zh_copy = remote(zh_out, zh_in, zh_sem.at[0], zh_sem.at[1], zh_peer)
    zh_copy.start()
    zh_copy.wait()
    other = unpack_stat(zh_in[BLOCK:, :])
    top = jnp.maximum(stat, other)
    here, there = jnp.exp2(stat - top), jnp.exp2(other - top)
    share_here, share_there = here / (here + there), there / (here + there)
    for j in range(GROUP):
        mixed = head_column(share_here, j) * means[j] + head_column(share_there, j) * zh_in[
            j * 16 : (j + 1) * 16, :
        ].astype(F32)
        attended[chip, j * 16 : (j + 1) * 16, :] = mixed.astype(BF16)

    def send_attended(i, _):
        remote(
            attended.at[chip], attended.at[chip], att_send.at[i], att_recv.at[chip],
            device(zh, plane_chip(i), core, head),
        ).start()
        return 0

    lax.fori_loop(1, 16, send_attended, 0)
    w_copy.wait_send()
    remote(weights.at[1 - core], weights.at[1 - core], w_sem.at[0], w_sem.at[1], sibling).wait_recv()

    def project(t, _):
        row_y = (y + t + t // 2 - 2 * (t // 3)) % 4
        head_of = core * 4 + row_y

        def arrive(i, _):
            source = row_y * 4 + i

            @pl.when(source != chip)
            def _():
                remote(
                    attended.at[source], attended.at[source], att_send.at[0], att_recv.at[source], sibling
                ).wait_recv()

            return 0

        lax.fori_loop(0, 4, arrive, 0)
        for side in range(2):
            acc = jnp.zeros((64, 128), F32)
            for j in range(GROUP):
                rows = attended[pl.ds(row_y * 4, 4), j * 16 : (j + 1) * 16, :].reshape(64, HD)
                acc += jnp.dot(rows, weights[side, j * HD : (j + 1) * HD, :], preferred_element_type=F32)
            proj_out[row_y, side] = acc.astype(BF16)
            mine = (head_of == head) & (core == side)

            @pl.when(mine)
            def _(side=side):
                proj_in[head] = proj_out[row_y, side]

            @pl.when(jnp.logical_not(mine))
            def _(side=side):
                remote(
                    proj_out.at[row_y, side], proj_in.at[head], proj_send.at[row_y, side], proj_recv.at[head],
                    device(zh, chip, side, head_of),
                ).start()

        return 0

    lax.fori_loop(0, 4, project, 0)

    def add_head(i, acc):
        @pl.when(jnp.logical_not((i == head) & (core == head // 4)))
        def _():
            remote(proj_in.at[i], proj_in.at[i], proj_send.at[0, 0], proj_recv.at[i], sibling).wait_recv()

        return acc + proj_in[i].astype(F32)

    result = lax.fori_loop(0, 8, add_head, jnp.zeros((64, 128), F32))
    out_ref[...] = result[:, :cols].astype(BF16)

    sib_copy.wait_send()

    def left_queries(i, _):
        for rel in range(2):
            remote(
                queries.at[rel, chip], queries.at[rel, chip], q_send.at[rel, i], q_recv.at[rel, chip], sibling
            ).wait_send()
        remote(attended.at[chip], attended.at[chip], att_send.at[i], att_recv.at[chip], sibling).wait_send()
        return 0

    lax.fori_loop(1, 16, left_queries, 0)

    def left_partials(i, _):
        for rel in range(2):

            @pl.when(jnp.logical_not((i == chip) & ((zh + rel) % 2 == core)))
            def _(rel=rel):
                remote(
                    partial.at[rel, i], landed.at[0], part_send.at[rel, i], part_recv.at[0], sibling
                ).wait_send()

        return 0

    lax.fori_loop(0, 16, left_partials, 0)

    def left_proj(i, _):
        for side in range(2):

            @pl.when(jnp.logical_not((core * 4 + i == head) & (core == side)))
            def _(side=side):
                remote(
                    proj_out.at[i, side], proj_in.at[0], proj_send.at[i, side], proj_recv.at[0], sibling
                ).wait_send()

        return 0

    lax.fori_loop(0, 4, left_proj, 0)


def shards(clean_query, noise, key_cache, value_cache, out_weight, row_run, limits, restored):
    shard_len, cols = key_cache.shape[0], out_weight.shape[1]
    vmem = pl.BlockSpec(memory_space=pltpu.VMEM)
    hbm = pl.BlockSpec(memory_space=pl.ANY)
    dma = pltpu.SemaphoreType.DMA
    return pl.pallas_call(
        kernel,
        out_shape=jax.ShapeDtypeStruct((64, cols), BF16),
        in_specs=[vmem, vmem, hbm, hbm, hbm, vmem, vmem, pl.BlockSpec(memory_space=pltpu.SMEM)],
        out_specs=vmem,
        scratch_shapes=[
            pltpu.VMEM((shard_len, HD), BF16),
            pltpu.VMEM((shard_len, HD), BF16),
            pltpu.VMEM(out_weight.shape, BF16),
            pltpu.VMEM((GROUP, 16, HD), F32),
            pltpu.VMEM((2, 16, BLOCK, HD), BF16),
            pltpu.VMEM((2 * HD, shard_len), BF16),
            pltpu.VMEM((shard_len, 2 * HD), BF16),
            pltpu.VMEM((CHUNK, 2 * HD), BF16),
            pltpu.VMEM((2, SUB, shard_len), F32),
            pltpu.VMEM((2, SUB, shard_len), BF16),
            pltpu.VMEM((2, SUB, 128), F32),
            pltpu.VMEM((2, 16, PACK, HD), BF16),
            pltpu.VMEM((32, PACK, HD), BF16),
            pltpu.VMEM((PACK, HD), BF16),
            pltpu.VMEM((PACK, HD), BF16),
            pltpu.VMEM((16, BLOCK, HD), BF16),
            pltpu.VMEM((2, GROUP * HD, 128), BF16),
            pltpu.VMEM((4, 2, 64, 128), BF16),
            pltpu.VMEM((8, 64, 128), BF16),
            pltpu.VMEM((512, 128), F32),
            pltpu.VMEM((512, 128), F32),
            dma((3,)),
            dma((2,)),
            dma((2,)),
            dma((2,)),
            dma((2, 16)),
            dma((2, 16)),
            dma((2, 16)),
            dma((32,)),
            dma((2,)),
            dma((16,)),
            dma((16,)),
            dma((4, 2)),
            dma((8,)),
        ],
        compiler_params=pltpu.CompilerParams(
            collective_id=0, has_side_effects=True, vmem_limit_bytes=40 << 20
        ),
        name="tracing",
    )(
        clean_query, noise, key_cache, value_cache, out_weight,
        row_run.reshape(4, 128), limits.reshape(4, 128), restored,
    )


def solution(mesh):
    placed = (
        P("seq", "head"),
        P("seq", "head"),
        P("seq", "head"),
        P("seq", "head"),
        P("head", "seq"),
        P(),
        P(),
        P(),
    )
    return jax.shard_map(
        shards, mesh=mesh, in_specs=placed, out_specs=P("head", "seq"), check_vma=False
    )
```

```python
import functools
import math

import jax
import jax.numpy as jnp
from jax import lax
from jax.experimental import pallas as pl
from jax.experimental.pallas import tpu as pltpu
from jax.sharding import PartitionSpec as P

MESH = pl.DeviceIdType.MESH
F32 = jnp.float32
BF16 = jnp.bfloat16

HD = 128
GROUP = 5
SCALE = math.log2(math.e) / math.sqrt(HD)
MASKED = -1e30
BLOCK = 16 * GROUP
PACK = BLOCK + 16
CHUNK = 4 * BLOCK
SUB = CHUNK // 2


def lanes_of(shape):
    return lax.broadcasted_iota(jnp.int32, shape, len(shape) - 1)


def pack_stat(rows):
    lane = lanes_of((16, 128))
    tile = jnp.zeros((16, 128), F32)
    for j, row in enumerate(rows):
        tile = jnp.where((lane % 8 == j) & (lane < 24), row, tile)
    high = tile.astype(BF16).astype(F32)
    rest = tile - high
    middle = rest.astype(BF16).astype(F32)
    low = rest - middle
    return jnp.where(lane < 8, high, jnp.where(lane < 16, middle, low)).astype(BF16)


def unpack_stat(tile):
    tile = tile.astype(F32)
    return tile + pltpu.roll(tile, 120, 1) + pltpu.roll(tile, 112, 1)


def head_column(tile, j):
    return jnp.broadcast_to(tile[:, j : j + 1], (16, 128))


def kernel(
    cq_ref, nz_ref, k_hbm, v_hbm, w_hbm, run_ref, lim_ref, restored_ref,
    out_ref,
    k_in, v_in, own_q, queries, rhs, v_ones, lhs, scores, probs, tops,
    partial, landed, zh_out, zh_in, attended, weights_t, weights, proj_out, proj_in, limit_col, share,
    load_sem, sib_sem, w_sem, zq_sem, q_send, q_recv, part_sem, zh_sem, att_send, att_recv, proj_sem,
):
    seq, head = lax.axis_index("seq"), lax.axis_index("head")
    shard_len = k_hbm.shape[0]
    cols = w_hbm.shape[0]
    zh, chip, core = seq // 32, (seq // 2) % 16, seq % 2
    y, x = chip // 4, chip % 4

    def device(zh_, chip_, core_, head_):
        return (zh_ * 32 + chip_ * 2 + core_, head_)

    def plane_chip(i):
        return lax.rem(y + i // 4, 4) * 4 + lax.rem(x + i % 4, 4)

    sibling = device(zh, chip, 1 - core, head)
    zh_peer = device(1 - zh, chip, core, head)

    def remote(src, dst, send, recv, to):
        return pltpu.make_async_remote_copy(
            src_ref=src, dst_ref=dst, send_sem=send, recv_sem=recv, device_id=to, device_id_type=MESH
        )

    barrier = pltpu.get_barrier_semaphore()

    def greet(to):
        pl.semaphore_signal(barrier, inc=1, device_id=to, device_id_type=MESH)

    greet(zh_peer)

    for i in (4, 3, 5, 2, 6, 1, 7):
        greet(device(zh, chip, core, lax.rem(head + i, 8)))
    for i in range(15, 0, -1):
        greet(device(zh, plane_chip(i), core, head))
    greet(sibling)

    for side in range(2):
        pad = slice(side * 128 + cols, (side + 1) * 128)
        weights_t[pad, :] = jnp.zeros((128 - cols, weights_t.shape[1]), BF16)
    my_cols = weights_t.at[pl.ds(pl.multiple_of(core * 128, 128), cols), :]
    their_cols = weights_t.at[pl.ds(pl.multiple_of(128 - core * 128, 128), cols), :]
    loads = [
        pltpu.make_async_copy(src, dst, load_sem.at[i])
        for i, (src, dst) in enumerate(((k_hbm, k_in), (v_hbm, v_in), (w_hbm, my_cols)))
    ]
    for load in loads:
        load.start()

    limits = lim_ref[pl.ds(seq // 16, 1), :]
    runs = run_ref[pl.ds(seq // 16, 1), :]
    restored = jnp.zeros(runs.shape, jnp.int32)
    for r in range(restored_ref.shape[0]):
        restored = jnp.where(runs == r, restored_ref[r], restored)
    keep = jnp.where(limits - 1 == restored, 0.0, 1.0).astype(F32)
    mine = lax.broadcasted_iota(jnp.int32, (8, 128), 0) + (seq % 16) * 8 == lanes_of((8, 128))
    my_keep = jnp.sum(jnp.where(mine, jnp.broadcast_to(keep, (8, 128)), 0.0), axis=1, keepdims=True)
    half_rows = pl.ds(pl.multiple_of(core * 8, 8), 8)
    for j in range(GROUP):
        at = slice(j * HD, (j + 1) * HD)
        own_q[j, half_rows, :] = cq_ref[:, at].astype(F32) + nz_ref[:, at].astype(F32) * my_keep

    loads[2].wait()

    pl.semaphore_wait(barrier, 24)

    sib_copy = remote(own_q.at[:, half_rows, :], own_q.at[:, half_rows, :], sib_sem.at[0], sib_sem.at[1], sibling)
    sib_copy.start()
    w_copy = remote(my_cols, my_cols, w_sem.at[0], w_sem.at[1], sibling)
    w_copy.start()
    other_rows = pl.ds(pl.multiple_of(8 - core * 8, 8), 8)
    remote(own_q.at[:, other_rows, :], own_q.at[:, other_rows, :], sib_sem.at[0], sib_sem.at[1], sibling).wait_recv()
    queries[0, chip] = own_q[...].reshape(BLOCK, HD).astype(BF16)
    zq_copy = remote(queries.at[0, chip], queries.at[1, chip], zq_sem.at[0], zq_sem.at[1], zh_peer)
    zq_copy.start()

    def send_queries(rel):
        for i in range(1, 16):
            remote(
                queries.at[rel, chip], queries.at[rel, chip], q_send.at[rel], q_recv.at[rel, y],
                device(zh, plane_chip(i), core, head),
            ).start()

    send_queries(0)

    limits = lim_ref[...].astype(F32)
    diagonal = lax.broadcasted_iota(jnp.int32, (128, 128), 0) == lanes_of((128, 128))
    for t in range(limits.shape[0]):
        spread = jnp.where(diagonal, jnp.broadcast_to(limits[t : t + 1, :], (128, 128)), 0.0)
        limit_col[t * 128 : (t + 1) * 128, :] = jnp.broadcast_to(jnp.sum(spread, axis=1, keepdims=True), (128, 128))
    row = lax.broadcasted_iota(jnp.int32, (CHUNK, 128), 0)
    one_hot = ((row // BLOCK) * 16 + row % 16) == lanes_of((CHUNK, 128))
    lhs[:, HD:] = jnp.where(one_hot, 1.0, 0.0).astype(BF16)
    rhs[HD + 64 :, :] = jnp.zeros((64, shard_len), BF16)
    v_ones[:, HD:] = jnp.ones((shard_len, HD), BF16)
    loads[0].wait()
    rhs[:HD, :] = k_in[...].T
    loads[1].wait()
    v_ones[:, :HD] = v_in[...]
    w_copy.wait_send()
    remote(their_cols, their_cols, w_sem.at[0], w_sem.at[1], sibling).wait_recv()
    weights[...] = weights_t[...].T

    start = (seq * shard_len).astype(F32)

    def chunk(g, _):
        rel, t = g // 4, (g + g // 4) % 4
        row_y = (y + t + t // 2 - 2 * (t // 3)) % 4
        zh_of = (zh + rel) % 2

        def arrive(count):
            some = queries.at[rel, pl.ds(0, count)]
            remote(some, some, q_send.at[rel], q_recv.at[rel, row_y], sibling).wait_recv()

        pl.when(t == 0)(lambda: arrive(3))
        pl.when(t != 0)(lambda: arrive(4))
        lhs[:, :HD] = queries[rel, pl.ds(row_y * 4, 4)].reshape(CHUNK, HD)
        first = pl.multiple_of(zh_of * 256 + row_y * 64, 64)
        limit = limit_col[pl.ds(first, 64), :] - start
        for at in range(0, shard_len, 128):
            position = (lanes_of((64, 128)) + at).astype(F32)
            rhs[HD : HD + 64, at : at + 128] = jnp.where(position < limit, 0.0, MASKED).astype(BF16)
        for i in range(4):
            if i < 2:
                scores[i] = jnp.dot(lhs[i * SUB : (i + 1) * SUB, :], rhs[...], preferred_element_type=F32)
            if 1 <= i < 3:
                part = scores[i - 1]
                top = jnp.max(part, axis=1, keepdims=True)
                tops[i - 1] = jnp.broadcast_to(top, (SUB, 128))
                probs[i - 1] = jnp.exp2((part - top) * SCALE).astype(BF16)
            if 2 <= i:
                both = jnp.dot(probs[i - 2], v_ones[...], preferred_element_type=F32)
                total = both[:, HD:]
                mean = (both[:, :HD] / total).astype(BF16)
                stat = tops[i - 2] * SCALE + jnp.log2(total)
                for b in range(2):
                    slot = row_y * 4 + (i - 2) * 2 + b
                    partial[rel * 16 + slot, :BLOCK, :] = mean[b * BLOCK : (b + 1) * BLOCK]
                    partial[rel * 16 + slot, BLOCK:, :] = pack_stat(
                        [stat[b * BLOCK + j * 16 : b * BLOCK + (j + 1) * 16] for j in range(GROUP)]
                    )

        def depart(i, _):
            owner = row_y * 4 + i
            mine = (owner == chip) & (zh_of == core)

            @pl.when(mine)
            def _():
                landed[seq % 32] = partial[rel * 16 + owner]

            @pl.when(jnp.logical_not(mine))
            def _():
                remote(
                    partial.at[rel * 16 + owner], landed.at[seq % 32], part_sem.at[0], part_sem.at[1],
                    device(zh, owner, zh_of, head),
                ).start()

            return 0

        lax.fori_loop(0, 4, depart, 0)
        return 0

    lax.fori_loop(0, 3, chunk, 0)
    zq_copy.wait()
    send_queries(1)
    lax.fori_loop(3, 8, chunk, 0)

    all_parts = remote(partial.at[pl.ds(0, 31)], landed.at[pl.ds(0, 31)], part_sem.at[0], part_sem.at[1], sibling)
    all_parts.wait_recv()
    stats = [unpack_stat(landed[i, BLOCK:, :]) for i in range(32)]
    top = functools.reduce(jnp.maximum, stats)
    shares = [jnp.exp2(stat - top) for stat in stats]
    total = sum(shares[1:], shares[0])
    for i in range(32):
        share[i] = shares[i]

    def gather_mean(step, sums):
        for k in range(8):
            i = step * 8 + k
            weight = share[i]
            sums = tuple(
                sums[j] + head_column(weight, j) * landed[i, j * 16 : (j + 1) * 16, :].astype(F32)
                for j in range(GROUP)
            )
        return sums

    sums = lax.fori_loop(0, 4, gather_mean, (jnp.zeros((16, 128), F32),) * GROUP)
    stat = top + jnp.log2(total)
    means = [sums[j] / head_column(total, j) for j in range(GROUP)]
    for j in range(GROUP):
        zh_out[j * 16 : (j + 1) * 16, :] = means[j].astype(BF16)
    zh_out[BLOCK:, :] = pack_stat([head_column(stat, j) for j in range(GROUP)])
    zh_copy = remote(zh_out, zh_in, zh_sem.at[0], zh_sem.at[1], zh_peer)
    zh_copy.start()
    zh_copy.wait()
    other = unpack_stat(zh_in[BLOCK:, :])
    top = jnp.maximum(stat, other)
    here, there = jnp.exp2(stat - top), jnp.exp2(other - top)
    share_here, share_there = here / (here + there), there / (here + there)
    for j in range(GROUP):
        mixed = head_column(share_here, j) * means[j] + head_column(share_there, j) * zh_in[
            j * 16 : (j + 1) * 16, :
        ].astype(F32)
        attended[chip, j * 16 : (j + 1) * 16, :] = mixed.astype(BF16)

    for i in range(1, 16):
        remote(
            attended.at[chip], attended.at[chip], att_send.at[0], att_recv.at[y],
            device(zh, plane_chip(i), core, head),
        ).start()

    def project(t, _):
        row_y = (y + t + t // 2 - 2 * (t // 3)) % 4
        head_of = core * 4 + row_y

        def arrive(count):
            some = attended.at[pl.ds(0, count)]
            remote(some, some, att_send.at[0], att_recv.at[row_y], sibling).wait_recv()

        pl.when(t == 0)(lambda: arrive(3))
        pl.when(t != 0)(lambda: arrive(4))
        rows = jnp.concatenate(
            [attended[pl.ds(row_y * 4, 4), j * 16 : (j + 1) * 16, :].reshape(64, HD) for j in range(GROUP)], axis=1
        )
        both = jnp.dot(rows, weights[...], preferred_element_type=F32).astype(BF16)
        for side in range(2):
            proj_out[row_y * 2 + side] = both[:, side * 128 : (side + 1) * 128]
            mine = (head_of == head) & (core == side)

            @pl.when(mine)
            def _(side=side):
                proj_in[head] = proj_out[row_y * 2 + side]

            @pl.when(jnp.logical_not(mine))
            def _(side=side):
                remote(
                    proj_out.at[row_y * 2 + side], proj_in.at[head], proj_sem.at[0], proj_sem.at[1],
                    device(zh, chip, side, head_of),
                ).start()

        return 0

    lax.fori_loop(0, 4, project, 0)

    def proj_wait(in_half, count):
        some, into = proj_out.at[pl.ds(0, count)], proj_in.at[pl.ds(0, count)]
        copy = remote(some, into, proj_sem.at[0], proj_sem.at[1], sibling)
        pl.when(in_half)(copy.wait_recv)
        return copy.wait_send

    in_half = core == head // 4
    left_seven = proj_wait(in_half, 7)
    left_eight = proj_wait(jnp.logical_not(in_half), 8)
    result = proj_in[0].astype(F32)
    for i in range(1, 8):
        result += proj_in[i].astype(F32)
    out_ref[...] = result[:, :cols].astype(BF16)

    sib_copy.wait_send()
    for rel in range(2):
        some = queries.at[rel, pl.ds(0, 15)]
        remote(some, some, q_send.at[rel], q_recv.at[rel, 0], sibling).wait_send()
    all_parts.wait_send()
    some = attended.at[pl.ds(0, 15)]
    remote(some, some, att_send.at[0], att_recv.at[0], sibling).wait_send()
    pl.when(in_half)(left_seven)
    pl.when(jnp.logical_not(in_half))(left_eight)


def shards(clean_query, noise, key_cache, value_cache, out_weight, row_run, limits, restored):
    shard_len, cols = key_cache.shape[0], out_weight.shape[1]
    vmem = pl.BlockSpec(memory_space=pltpu.VMEM)
    hbm = pl.BlockSpec(memory_space=pltpu.HBM)
    dma = pltpu.SemaphoreType.DMA
    return pl.pallas_call(
        kernel,
        out_shape=jax.ShapeDtypeStruct((64, cols), BF16),
        in_specs=[vmem, vmem, hbm, hbm, hbm, vmem, vmem, pl.BlockSpec(memory_space=pltpu.SMEM)],
        out_specs=vmem,
        scratch_shapes=[
            pltpu.VMEM((shard_len, HD), BF16),
            pltpu.VMEM((shard_len, HD), BF16),
            pltpu.VMEM((GROUP, 16, HD), F32),
            pltpu.VMEM((2, 16, BLOCK, HD), BF16),
            pltpu.VMEM((2 * HD, shard_len), BF16),
            pltpu.VMEM((shard_len, 2 * HD), BF16),
            pltpu.VMEM((CHUNK, 2 * HD), BF16),
            pltpu.VMEM((2, SUB, shard_len), F32),
            pltpu.VMEM((2, SUB, shard_len), BF16),
            pltpu.VMEM((2, SUB, 128), F32),
            pltpu.VMEM((32, PACK, HD), BF16),
            pltpu.VMEM((32, PACK, HD), BF16),
            pltpu.VMEM((PACK, HD), BF16),
            pltpu.VMEM((PACK, HD), BF16),
            pltpu.VMEM((16, BLOCK, HD), BF16),
            pltpu.VMEM((256, GROUP * HD), BF16),
            pltpu.VMEM((GROUP * HD, 256), BF16),
            pltpu.VMEM((8, 64, 128), BF16),
            pltpu.VMEM((8, 64, 128), BF16),
            pltpu.VMEM((512, 128), F32),
            pltpu.VMEM((32, 16, 128), F32),
            dma((3,)),
            dma((2,)),
            dma((2,)),
            dma((2,)),
            dma((2,)),
            dma((2, 4)),
            dma((2,)),
            dma((2,)),
            dma((1,)),
            dma((4,)),
            dma((2,)),
        ],
        compiler_params=pltpu.CompilerParams(
            collective_id=0, has_side_effects=True, vmem_limit_bytes=60 << 20
        ),
        name="tracing",
    )(
        clean_query, noise, key_cache, value_cache, out_weight.T,
        row_run.reshape(4, 128), limits.reshape(4, 128), restored,
    )


def solution(mesh):
    placed = (
        P("seq", "head"),
        P("seq", "head"),
        P("seq", "head"),
        P("seq", "head"),
        P("head", "seq"),
        P(),
        P(),
        P(),
    )
    return jax.shard_map(
        shards, mesh=mesh, in_specs=placed, out_specs=P("head", "seq"), check_vma=False
    )
```

```python
import functools
import math

import jax
import jax.numpy as jnp
from jax import lax
from jax.experimental import pallas as pl
from jax.experimental.pallas import tpu as pltpu
from jax.sharding import PartitionSpec as P

MESH = pl.DeviceIdType.MESH
F32 = jnp.float32
BF16 = jnp.bfloat16

HD = 128
GROUP = 5
SCALE = math.log2(math.e) / math.sqrt(HD)
MASKED = -1e30
BLOCK = 16 * GROUP
PACK = BLOCK + 16
CHUNK = 4 * BLOCK
SUB = CHUNK // 2


def lanes_of(shape):
    return lax.broadcasted_iota(jnp.int32, shape, len(shape) - 1)


def pack_stat(rows):
    lane = lanes_of((16, 128))
    tile = jnp.zeros((16, 128), F32)
    for j, row in enumerate(rows):
        tile = jnp.where((lane % 8 == j) & (lane < 24), row, tile)
    high = tile.astype(BF16).astype(F32)
    rest = tile - high
    middle = rest.astype(BF16).astype(F32)
    low = rest - middle
    return jnp.where(lane < 8, high, jnp.where(lane < 16, middle, low)).astype(BF16)


def unpack_stat(tile):
    tile = tile.astype(F32)
    return tile + pltpu.roll(tile, 120, 1) + pltpu.roll(tile, 112, 1)


def head_column(tile, j):
    return jnp.broadcast_to(tile[:, j : j + 1], (16, 128))


def kernel(
    cq_ref, nz_ref, k_hbm, v_hbm, w_hbm, run_ref, lim_ref, restored_ref,
    out_ref,
    k_in, v_in, own_q, far_q, queries, rhs, v_ones, lhs, scores, probs, tops,
    partial, landed, zh_out, zh_in, attended, weights_t, weights, proj_out, proj_in, limit_col, share,
    load_sem, sib_sem, w_sem, zq_send, zq_recv, q_send, q_recv, part_sem, zh_sem, att_send, att_recv, proj_sem,
):
    seq, head = lax.axis_index("seq"), lax.axis_index("head")
    shard_len = k_hbm.shape[0]
    cols = w_hbm.shape[0]
    zh, chip, core = seq // 32, (seq // 2) % 16, seq % 2
    y, x = chip // 4, chip % 4

    def device(zh_, chip_, core_, head_):
        return (zh_ * 32 + chip_ * 2 + core_, head_)

    def plane_chip(i):
        return lax.rem(y + i // 4, 4) * 4 + lax.rem(x + i % 4, 4)

    sibling = device(zh, chip, 1 - core, head)
    zh_peer = device(1 - zh, chip, core, head)

    def remote(src, dst, send, recv, to):
        return pltpu.make_async_remote_copy(
            src_ref=src, dst_ref=dst, send_sem=send, recv_sem=recv, device_id=to, device_id_type=MESH
        )

    barrier = pltpu.get_barrier_semaphore()

    def greet(to):
        pl.semaphore_signal(barrier, inc=1, device_id=to, device_id_type=MESH)

    greet(zh_peer)
    greet(device(1 - zh, chip, 1 - core, head))

    for i in (4, 3, 5, 2, 6, 1, 7):
        greet(device(zh, chip, core, lax.rem(head + i, 8)))
    for i in range(15, 0, -1):
        greet(device(zh, plane_chip(i), core, head))
    greet(sibling)

    for side in range(2):
        pad = slice(side * 128 + cols, (side + 1) * 128)
        weights_t[pad, :] = jnp.zeros((128 - cols, weights_t.shape[1]), BF16)
    my_cols = weights_t.at[pl.ds(pl.multiple_of(core * 128, 128), cols), :]
    their_cols = weights_t.at[pl.ds(pl.multiple_of(128 - core * 128, 128), cols), :]
    loads = [
        pltpu.make_async_copy(src, dst, load_sem.at[i])
        for i, (src, dst) in enumerate(((k_hbm, k_in), (v_hbm, v_in), (w_hbm, my_cols)))
    ]
    for load in loads:
        load.start()

    limits = lim_ref[pl.ds(seq // 16, 1), :]
    runs = run_ref[pl.ds(seq // 16, 1), :]
    restored = jnp.zeros(runs.shape, jnp.int32)
    for r in range(restored_ref.shape[0]):
        restored = jnp.where(runs == r, restored_ref[r], restored)
    keep = jnp.where(limits - 1 == restored, 0.0, 1.0).astype(F32)
    mine = lax.broadcasted_iota(jnp.int32, (8, 128), 0) + (seq % 16) * 8 == lanes_of((8, 128))
    my_keep = jnp.sum(jnp.where(mine, jnp.broadcast_to(keep, (8, 128)), 0.0), axis=1, keepdims=True)
    half = 3 * HD
    mixed = cq_ref[...].astype(F32) + nz_ref[...].astype(F32) * my_keep
    rest = jnp.concatenate([mixed[:, half:], jnp.zeros((8, 2 * half - GROUP * HD), F32)], axis=1)
    own_q[core] = jnp.concatenate([mixed[:, :half], rest], axis=0).astype(BF16)

    loads[2].wait()

    pl.semaphore_wait(barrier, 25)

    zh_copies = [
        remote(own_q.at[core], far_q.at[core], zq_send.at[side], zq_recv.at[core], device(1 - zh, chip, side, head))
        for side in range(2)
    ]
    for copy in zh_copies:
        copy.start()
    sib_copy = remote(own_q.at[core], own_q.at[core], sib_sem.at[0], sib_sem.at[1], sibling)
    sib_copy.start()
    w_copy = remote(my_cols, my_cols, w_sem.at[0], w_sem.at[1], sibling)
    w_copy.start()

    def assemble(rel, pair):
        for j in range(GROUP):
            at = (slice(j // 3 * 8, j // 3 * 8 + 8), slice(j % 3 * HD, j % 3 * HD + HD))
            rows = jnp.concatenate([pair[k][at].astype(F32) for k in range(2)], axis=0)
            queries[rel, chip, j * 16 : (j + 1) * 16, :] = rows.astype(BF16)

    remote(own_q.at[1 - core], own_q.at[1 - core], sib_sem.at[0], sib_sem.at[1], sibling).wait_recv()
    assemble(0, [own_q[0], own_q[1]])

    def send_queries(rel):
        for i in range(1, 16):
            remote(
                queries.at[rel, chip], queries.at[rel, chip], q_send.at[rel], q_recv.at[rel, y],
                device(zh, plane_chip(i), core, head),
            ).start()

    send_queries(0)

    limits = lim_ref[...].astype(F32)
    diagonal = lax.broadcasted_iota(jnp.int32, (128, 128), 0) == lanes_of((128, 128))
    for t in range(limits.shape[0]):
        spread = jnp.where(diagonal, jnp.broadcast_to(limits[t : t + 1, :], (128, 128)), 0.0)
        limit_col[t * 128 : (t + 1) * 128, :] = jnp.broadcast_to(jnp.sum(spread, axis=1, keepdims=True), (128, 128))
    row = lax.broadcasted_iota(jnp.int32, (CHUNK, 128), 0)
    one_hot = ((row // BLOCK) * 16 + row % 16) == lanes_of((CHUNK, 128))
    lhs[:, HD:] = jnp.where(one_hot, 1.0, 0.0).astype(BF16)
    rhs[HD + 64 :, :] = jnp.zeros((64, shard_len), BF16)
    v_ones[:, HD:] = jnp.ones((shard_len, HD), BF16)
    loads[0].wait()
    rhs[:HD, :] = k_in[...].T
    loads[1].wait()
    v_ones[:, :HD] = v_in[...]
    w_copy.wait_send()
    remote(their_cols, their_cols, w_sem.at[0], w_sem.at[1], sibling).wait_recv()
    weights[...] = weights_t[...].T

    start = (seq * shard_len).astype(F32)

    def chunk(g, _):
        rel, t = g // 4, g % 4
        row_y = (y + t + t // 2 - 2 * (t // 3)) % 4
        zh_of = (zh + rel) % 2

        def arrive(count):
            some = queries.at[rel, pl.ds(0, count)]
            remote(some, some, q_send.at[rel], q_recv.at[rel, row_y], sibling).wait_recv()

        pl.when(t == 0)(lambda: arrive(3))
        pl.when(t != 0)(lambda: arrive(4))
        lhs[:, :HD] = queries[rel, pl.ds(row_y * 4, 4)].reshape(CHUNK, HD)
        first = pl.multiple_of(zh_of * 256 + row_y * 64, 64)
        limit = limit_col[pl.ds(first, 64), :] - start
        for at in range(0, shard_len, 128):
            position = (lanes_of((64, 128)) + at).astype(F32)
            rhs[HD : HD + 64, at : at + 128] = jnp.where(position < limit, 0.0, MASKED).astype(BF16)
        for i in range(4):
            if i < 2:
                scores[i] = jnp.dot(lhs[i * SUB : (i + 1) * SUB, :], rhs[...], preferred_element_type=F32)
            if 1 <= i < 3:
                part = scores[i - 1]
                top = jnp.max(part, axis=1, keepdims=True)
                tops[i - 1] = jnp.broadcast_to(top, (SUB, 128))
                probs[i - 1] = jnp.exp2((part - top) * SCALE).astype(BF16)
            if 2 <= i:
                both = jnp.dot(probs[i - 2], v_ones[...], preferred_element_type=F32)
                total = both[:, HD:]
                mean = (both[:, :HD] / total).astype(BF16)
                stat = tops[i - 2] * SCALE + jnp.log2(total)
                for b in range(2):
                    slot = row_y * 4 + (i - 2) * 2 + b
                    partial[rel * 16 + slot, :BLOCK, :] = mean[b * BLOCK : (b + 1) * BLOCK]
                    partial[rel * 16 + slot, BLOCK:, :] = pack_stat(
                        [stat[b * BLOCK + j * 16 : b * BLOCK + (j + 1) * 16] for j in range(GROUP)]
                    )

        def depart(i, _):
            owner = row_y * 4 + i
            mine = (owner == chip) & (zh_of == core)

            @pl.when(mine)
            def _():
                landed[seq % 32] = partial[rel * 16 + owner]

            @pl.when(jnp.logical_not(mine))
            def _():
                remote(
                    partial.at[rel * 16 + owner], landed.at[seq % 32], part_sem.at[0], part_sem.at[1],
                    device(zh, owner, zh_of, head),
                ).start()

            return 0

        lax.fori_loop(0, 4, depart, 0)
        return 0

    for side in range(2):
        remote(far_q.at[side], far_q.at[side], zq_send.at[side], zq_recv.at[side], sibling).wait_recv()
    assemble(1, [far_q[0], far_q[1]])
    send_queries(1)
    lax.fori_loop(0, 8, chunk, 0)

    all_parts = remote(partial.at[pl.ds(0, 31)], landed.at[pl.ds(0, 31)], part_sem.at[0], part_sem.at[1], sibling)
    all_parts.wait_recv()
    stats = [unpack_stat(landed[i, BLOCK:, :]) for i in range(32)]
    top = functools.reduce(jnp.maximum, stats)
    shares = [jnp.exp2(stat - top) for stat in stats]
    total = sum(shares[1:], shares[0])
    for i in range(32):
        share[i] = shares[i]

    def gather_mean(step, sums):
        for k in range(8):
            i = step * 8 + k
            weight = share[i]
            sums = tuple(
                sums[j] + head_column(weight, j) * landed[i, j * 16 : (j + 1) * 16, :].astype(F32)
                for j in range(GROUP)
            )
        return sums

    sums = lax.fori_loop(0, 4, gather_mean, (jnp.zeros((16, 128), F32),) * GROUP)
    stat = top + jnp.log2(total)
    means = [sums[j] / head_column(total, j) for j in range(GROUP)]
    for j in range(GROUP):
        zh_out[j * 16 : (j + 1) * 16, :] = means[j].astype(BF16)
    zh_out[BLOCK:, :] = pack_stat([head_column(stat, j) for j in range(GROUP)])
    zh_copy = remote(zh_out, zh_in, zh_sem.at[0], zh_sem.at[1], zh_peer)
    zh_copy.start()
    zh_copy.wait()
    other = unpack_stat(zh_in[BLOCK:, :])
    top = jnp.maximum(stat, other)
    here, there = jnp.exp2(stat - top), jnp.exp2(other - top)
    share_here, share_there = here / (here + there), there / (here + there)
    for j in range(GROUP):
        mixed = head_column(share_here, j) * means[j] + head_column(share_there, j) * zh_in[
            j * 16 : (j + 1) * 16, :
        ].astype(F32)
        attended[chip, j * 16 : (j + 1) * 16, :] = mixed.astype(BF16)

    for i in range(1, 16):
        remote(
            attended.at[chip], attended.at[chip], att_send.at[0], att_recv.at[y],
            device(zh, plane_chip(i), core, head),
        ).start()

    def project(t, _):
        row_y = (y + t + t // 2 - 2 * (t // 3)) % 4
        head_of = core * 4 + row_y

        def arrive(count):
            some = attended.at[pl.ds(0, count)]
            remote(some, some, att_send.at[0], att_recv.at[row_y], sibling).wait_recv()

        pl.when(t == 0)(lambda: arrive(3))
        pl.when(t != 0)(lambda: arrive(4))
        rows = jnp.concatenate(
            [attended[pl.ds(row_y * 4, 4), j * 16 : (j + 1) * 16, :].reshape(64, HD) for j in range(GROUP)], axis=1
        )
        both = jnp.dot(rows, weights[...], preferred_element_type=F32).astype(BF16)
        for side in range(2):
            proj_out[row_y * 2 + side] = both[:, side * 128 : (side + 1) * 128]
            mine = (head_of == head) & (core == side)

            @pl.when(mine)
            def _(side=side):
                proj_in[head] = proj_out[row_y * 2 + side]

            @pl.when(jnp.logical_not(mine))
            def _(side=side):
                remote(
                    proj_out.at[row_y * 2 + side], proj_in.at[head], proj_sem.at[0], proj_sem.at[1],
                    device(zh, chip, side, head_of),
                ).start()

        return 0

    lax.fori_loop(0, 4, project, 0)

    def proj_wait(in_half, count):
        some, into = proj_out.at[pl.ds(0, count)], proj_in.at[pl.ds(0, count)]
        copy = remote(some, into, proj_sem.at[0], proj_sem.at[1], sibling)
        pl.when(in_half)(copy.wait_recv)
        return copy.wait_send

    in_half = core == head // 4
    left_seven = proj_wait(in_half, 7)
    left_eight = proj_wait(jnp.logical_not(in_half), 8)
    result = proj_in[0].astype(F32)
    for i in range(1, 8):
        result += proj_in[i].astype(F32)
    out_ref[...] = result[:, :cols].astype(BF16)

    sib_copy.wait_send()
    for copy in zh_copies:
        copy.wait_send()
    for rel in range(2):
        some = queries.at[rel, pl.ds(0, 15)]
        remote(some, some, q_send.at[rel], q_recv.at[rel, 0], sibling).wait_send()
    all_parts.wait_send()
    some = attended.at[pl.ds(0, 15)]
    remote(some, some, att_send.at[0], att_recv.at[0], sibling).wait_send()
    pl.when(in_half)(left_seven)
    pl.when(jnp.logical_not(in_half))(left_eight)


def shards(clean_query, noise, key_cache, value_cache, out_weight, row_run, limits, restored):
    shard_len, cols = key_cache.shape[0], out_weight.shape[1]
    vmem = pl.BlockSpec(memory_space=pltpu.VMEM)
    hbm = pl.BlockSpec(memory_space=pltpu.HBM)
    dma = pltpu.SemaphoreType.DMA
    return pl.pallas_call(
        kernel,
        out_shape=jax.ShapeDtypeStruct((64, cols), BF16),
        in_specs=[vmem, vmem, hbm, hbm, hbm, vmem, vmem, pl.BlockSpec(memory_space=pltpu.SMEM)],
        out_specs=vmem,
        scratch_shapes=[
            pltpu.VMEM((shard_len, HD), BF16),
            pltpu.VMEM((shard_len, HD), BF16),
            pltpu.VMEM((2, 16, 3 * HD), BF16),
            pltpu.VMEM((2, 16, 3 * HD), BF16),
            pltpu.VMEM((2, 16, BLOCK, HD), BF16),
            pltpu.VMEM((2 * HD, shard_len), BF16),
            pltpu.VMEM((shard_len, 2 * HD), BF16),
            pltpu.VMEM((CHUNK, 2 * HD), BF16),
            pltpu.VMEM((2, SUB, shard_len), F32),
            pltpu.VMEM((2, SUB, shard_len), BF16),
            pltpu.VMEM((2, SUB, 128), F32),
            pltpu.VMEM((32, PACK, HD), BF16),
            pltpu.VMEM((32, PACK, HD), BF16),
            pltpu.VMEM((PACK, HD), BF16),
            pltpu.VMEM((PACK, HD), BF16),
            pltpu.VMEM((16, BLOCK, HD), BF16),
            pltpu.VMEM((256, GROUP * HD), BF16),
            pltpu.VMEM((GROUP * HD, 256), BF16),
            pltpu.VMEM((8, 64, 128), BF16),
            pltpu.VMEM((8, 64, 128), BF16),
            pltpu.VMEM((512, 128), F32),
            pltpu.VMEM((32, 16, 128), F32),
            dma((3,)),
            dma((2,)),
            dma((2,)),
            dma((2,)),
            dma((2,)),
            dma((2,)),
            dma((2, 4)),
            dma((2,)),
            dma((2,)),
            dma((1,)),
            dma((4,)),
            dma((2,)),
        ],
        compiler_params=pltpu.CompilerParams(
            collective_id=0, has_side_effects=True, vmem_limit_bytes=60 << 20
        ),
        name="tracing",
    )(
        clean_query, noise, key_cache, value_cache, out_weight.T,
        row_run.reshape(4, 128), limits.reshape(4, 128), restored,
    )


def solution(mesh):
    placed = (
        P("seq", "head"),
        P("seq", "head"),
        P("seq", "head"),
        P("seq", "head"),
        P("head", "seq"),
        P(),
        P(),
        P(),
    )
    return jax.shard_map(
        shards, mesh=mesh, in_specs=placed, out_specs=P("head", "seq"), check_vma=False
    )
```

```python
import functools
import math

import jax
import jax.numpy as jnp
from jax import lax
from jax.experimental import pallas as pl
from jax.experimental.pallas import tpu as pltpu
from jax.sharding import PartitionSpec as P

MESH = pl.DeviceIdType.MESH
F32 = jnp.float32
BF16 = jnp.bfloat16

HD = 128
GROUP = 5
SCALE = math.log2(math.e) / math.sqrt(HD)
MASKED = -1e30
BLOCK = 16 * GROUP
PACK = BLOCK + 16
CHUNK = 4 * BLOCK
SUB = CHUNK // 2


def lanes_of(shape):
    return lax.broadcasted_iota(jnp.int32, shape, len(shape) - 1)


def pack_stat(rows):
    lane = lanes_of((16, 128))
    tile = jnp.zeros((16, 128), F32)
    for j, row in enumerate(rows):
        tile = jnp.where((lane % 8 == j) & (lane < 24), row, tile)
    high = tile.astype(BF16).astype(F32)
    rest = tile - high
    middle = rest.astype(BF16).astype(F32)
    low = rest - middle
    return jnp.where(lane < 8, high, jnp.where(lane < 16, middle, low)).astype(BF16)


def unpack_stat(tile):
    tile = tile.astype(F32)
    return tile + pltpu.roll(tile, 120, 1) + pltpu.roll(tile, 112, 1)


def head_column(tile, j):
    return jnp.broadcast_to(tile[:, j : j + 1], (16, 128))


def kernel(
    cq_ref, nz_ref, k_hbm, v_hbm, w_hbm, run_ref, lim_ref, restored_ref,
    out_ref,
    k_in, v_in, own_q, far_q, queries, rhs, v_ones, lhs, scores, probs, tops,
    partial, landed, zh_out, zh_in, attended, weights_t, weights, proj_out, proj_in, limit_col, share,
    load_sem, sib_sem, w_sem, zq_send, zq_recv, q_send, q_recv, part_sem, zh_sem, att_send, att_recv, proj_sem,
):
    seq, head = lax.axis_index("seq"), lax.axis_index("head")
    shard_len = k_hbm.shape[0]
    cols = w_hbm.shape[0]
    zh, chip, core = seq // 32, (seq // 2) % 16, seq % 2
    y, x = chip // 4, chip % 4

    def device(zh_, chip_, core_, head_):
        return (zh_ * 32 + chip_ * 2 + core_, head_)

    def plane_chip(i):
        return lax.rem(y + i // 4, 4) * 4 + lax.rem(x + i % 4, 4)

    sibling = device(zh, chip, 1 - core, head)
    zh_peer = device(1 - zh, chip, core, head)

    def remote(src, dst, send, recv, to):
        return pltpu.make_async_remote_copy(
            src_ref=src, dst_ref=dst, send_sem=send, recv_sem=recv, device_id=to, device_id_type=MESH
        )

    barrier = pltpu.get_barrier_semaphore()

    def greet(to):
        pl.semaphore_signal(barrier, inc=1, device_id=to, device_id_type=MESH)

    greet(zh_peer)
    greet(device(1 - zh, chip, 1 - core, head))

    for i in (4, 3, 5, 2, 6, 1, 7):
        greet(device(zh, chip, core, lax.rem(head + i, 8)))
    for i in range(15, 0, -1):
        greet(device(zh, plane_chip(i), core, head))
    greet(sibling)

    for side in range(2):
        pad = slice(side * 128 + cols, (side + 1) * 128)
        weights_t[pad, :] = jnp.zeros((128 - cols, weights_t.shape[1]), BF16)
    my_cols = weights_t.at[pl.ds(pl.multiple_of(core * 128, 128), cols), :]
    their_cols = weights_t.at[pl.ds(pl.multiple_of(128 - core * 128, 128), cols), :]
    loads = [
        pltpu.make_async_copy(src, dst, load_sem.at[i])
        for i, (src, dst) in enumerate(((k_hbm, k_in), (v_hbm, v_in), (w_hbm, my_cols)))
    ]
    for load in loads:
        load.start()

    limits = lim_ref[pl.ds(seq // 16, 1), :]
    runs = run_ref[pl.ds(seq // 16, 1), :]
    restored = jnp.zeros(runs.shape, jnp.int32)
    for r in range(restored_ref.shape[0]):
        restored = jnp.where(runs == r, restored_ref[r], restored)
    keep = jnp.where(limits - 1 == restored, 0.0, 1.0).astype(F32)
    mine = lax.broadcasted_iota(jnp.int32, (8, 128), 0) + (seq % 16) * 8 == lanes_of((8, 128))
    my_keep = jnp.sum(jnp.where(mine, jnp.broadcast_to(keep, (8, 128)), 0.0), axis=1, keepdims=True)
    half = 3 * HD
    mixed = cq_ref[...].astype(F32) + nz_ref[...].astype(F32) * my_keep
    rest = jnp.concatenate([mixed[:, half:], jnp.zeros((8, 2 * half - GROUP * HD), F32)], axis=1)
    own_q[core] = jnp.concatenate([mixed[:, :half], rest], axis=0).astype(BF16)

    loads[2].wait()

    pl.semaphore_wait(barrier, 25)

    zh_copies = [
        remote(own_q.at[core], far_q.at[core], zq_send.at[side], zq_recv.at[core], device(1 - zh, chip, side, head))
        for side in range(2)
    ]
    for copy in zh_copies:
        copy.start()
    sib_copy = remote(own_q.at[core], own_q.at[core], sib_sem.at[0], sib_sem.at[1], sibling)
    sib_copy.start()
    w_copy = remote(my_cols, my_cols, w_sem.at[0], w_sem.at[1], sibling)
    w_copy.start()

    def assemble(rel, pair):
        for j in range(GROUP):
            at = (slice(j // 3 * 8, j // 3 * 8 + 8), slice(j % 3 * HD, j % 3 * HD + HD))
            rows = jnp.concatenate([pair[k][at].astype(F32) for k in range(2)], axis=0)
            queries[rel, chip, j * 16 : (j + 1) * 16, :] = rows.astype(BF16)

    remote(own_q.at[1 - core], own_q.at[1 - core], sib_sem.at[0], sib_sem.at[1], sibling).wait_recv()
    assemble(0, [own_q[0], own_q[1]])

    def send_queries(rel):
        for i in range(1, 16):
            remote(
                queries.at[rel, chip], queries.at[rel, chip], q_send.at[rel], q_recv.at[rel, y],
                device(zh, plane_chip(i), core, head),
            ).start()

    send_queries(0)

    limits = lim_ref[...].astype(F32)
    diagonal = lax.broadcasted_iota(jnp.int32, (128, 128), 0) == lanes_of((128, 128))
    for t in range(limits.shape[0]):
        spread = jnp.where(diagonal, jnp.broadcast_to(limits[t : t + 1, :], (128, 128)), 0.0)
        limit_col[t * 128 : (t + 1) * 128, :] = jnp.broadcast_to(jnp.sum(spread, axis=1, keepdims=True), (128, 128))
    row = lax.broadcasted_iota(jnp.int32, (CHUNK, 128), 0)
    one_hot = ((row // BLOCK) * 16 + row % 16) == lanes_of((CHUNK, 128))
    lhs[:, HD:] = jnp.where(one_hot, 1.0, 0.0).astype(BF16)
    rhs[HD + 64 :, :] = jnp.zeros((64, shard_len), BF16)
    v_ones[:, HD:] = jnp.ones((shard_len, HD), BF16)
    loads[0].wait()
    rhs[:HD, :] = k_in[...].T
    loads[1].wait()
    v_ones[:, :HD] = v_in[...]
    w_copy.wait_send()
    remote(their_cols, their_cols, w_sem.at[0], w_sem.at[1], sibling).wait_recv()
    weights[...] = weights_t[...].T

    start = (seq * shard_len).astype(F32)

    def chunk(g, _):
        rel, t = g // 4, g % 4
        row_y = (y + t + t // 2 - 2 * (t // 3)) % 4
        zh_of = (zh + rel) % 2

        def arrive(count):
            some = queries.at[rel, pl.ds(0, count)]
            remote(some, some, q_send.at[rel], q_recv.at[rel, row_y], sibling).wait_recv()

        pl.when(t == 0)(lambda: arrive(3))
        pl.when(t != 0)(lambda: arrive(4))
        lhs[:, :HD] = queries[rel, pl.ds(row_y * 4, 4)].reshape(CHUNK, HD)
        first = pl.multiple_of(zh_of * 256 + row_y * 64, 64)
        limit = limit_col[pl.ds(first, 64), :] - start
        for at in range(0, shard_len, 128):
            position = (lanes_of((64, 128)) + at).astype(F32)
            rhs[HD : HD + 64, at : at + 128] = jnp.where(position < limit, 0.0, MASKED).astype(BF16)
        for i in range(4):
            if i < 2:
                scores[i] = jnp.dot(lhs[i * SUB : (i + 1) * SUB, :], rhs[...], preferred_element_type=F32)
            if 1 <= i < 3:
                part = scores[i - 1]
                top = jnp.max(part, axis=1, keepdims=True)
                tops[i - 1] = jnp.broadcast_to(top, (SUB, 128))
                probs[i - 1] = jnp.exp2((part - top) * SCALE).astype(BF16)
            if 2 <= i:
                both = jnp.dot(probs[i - 2], v_ones[...], preferred_element_type=F32)
                total = both[:, HD:]
                mean = (both[:, :HD] / total).astype(BF16)
                stat = tops[i - 2] * SCALE + jnp.log2(total)
                for b in range(2):
                    slot = row_y * 4 + (i - 2) * 2 + b
                    partial[rel * 16 + slot, :BLOCK, :] = mean[b * BLOCK : (b + 1) * BLOCK]
                    partial[rel * 16 + slot, BLOCK:, :] = pack_stat(
                        [stat[b * BLOCK + j * 16 : b * BLOCK + (j + 1) * 16] for j in range(GROUP)]
                    )

        def depart(i, _):
            owner = row_y * 4 + i
            mine = (owner == chip) & (zh_of == core)

            @pl.when(mine)
            def _():
                landed[seq % 32] = partial[rel * 16 + owner]

            @pl.when(jnp.logical_not(mine))
            def _():
                remote(
                    partial.at[rel * 16 + owner], landed.at[seq % 32], part_sem.at[0], part_sem.at[1],
                    device(zh, owner, zh_of, head),
                ).start()

            return 0

        lax.fori_loop(0, 4, depart, 0)
        return 0

    for side in range(2):
        remote(far_q.at[side], far_q.at[side], zq_send.at[side], zq_recv.at[side], sibling).wait_recv()
    assemble(1, [far_q[0], far_q[1]])
    send_queries(1)
    lax.fori_loop(0, 8, chunk, 0)

    all_parts = remote(partial.at[pl.ds(0, 31)], landed.at[pl.ds(0, 31)], part_sem.at[0], part_sem.at[1], sibling)
    all_parts.wait_recv()
    stats = [unpack_stat(landed[i, BLOCK:, :]) for i in range(32)]
    top = functools.reduce(jnp.maximum, stats)
    shares = [jnp.exp2(stat - top) for stat in stats]
    total = sum(shares[1:], shares[0])
    for i in range(32):
        share[i] = shares[i]

    def gather_mean(step, sums):
        for k in range(8):
            i = step * 8 + k
            weight = share[i]
            sums = tuple(
                sums[j] + head_column(weight, j) * landed[i, j * 16 : (j + 1) * 16, :].astype(F32)
                for j in range(GROUP)
            )
        return sums

    sums = lax.fori_loop(0, 4, gather_mean, (jnp.zeros((16, 128), F32),) * GROUP)
    stat = top + jnp.log2(total)
    means = [sums[j] / head_column(total, j) for j in range(GROUP)]
    for j in range(GROUP):
        zh_out[j * 16 : (j + 1) * 16, :] = means[j].astype(BF16)
    zh_out[BLOCK:, :] = pack_stat([head_column(stat, j) for j in range(GROUP)])
    zh_copy = remote(zh_out, zh_in, zh_sem.at[0], zh_sem.at[1], zh_peer)
    zh_copy.start()
    zh_copy.wait()
    other = unpack_stat(zh_in[BLOCK:, :])
    top = jnp.maximum(stat, other)
    here, there = jnp.exp2(stat - top), jnp.exp2(other - top)
    share_here, share_there = here / (here + there), there / (here + there)
    for j in range(GROUP):
        mixed = head_column(share_here, j) * means[j] + head_column(share_there, j) * zh_in[
            j * 16 : (j + 1) * 16, :
        ].astype(F32)
        attended[chip, j * 16 : (j + 1) * 16, :] = mixed.astype(BF16)

    for i in range(15, 0, -1):
        remote(
            attended.at[chip], attended.at[chip], att_send.at[0], att_recv.at[y],
            device(zh, plane_chip(i), core, head),
        ).start()

    def project(t, _):
        row_y = (y + t + t // 2 - 2 * (t // 3)) % 4
        head_of = core * 4 + row_y

        def arrive(count):
            some = attended.at[pl.ds(0, count)]
            remote(some, some, att_send.at[0], att_recv.at[row_y], sibling).wait_recv()

        pl.when(t == 0)(lambda: arrive(3))
        pl.when(t != 0)(lambda: arrive(4))
        rows = jnp.concatenate(
            [attended[pl.ds(row_y * 4, 4), j * 16 : (j + 1) * 16, :].reshape(64, HD) for j in range(GROUP)], axis=1
        )
        both = jnp.dot(rows, weights[...], preferred_element_type=F32).astype(BF16)
        for side in range(2):
            proj_out[row_y * 2 + side] = both[:, side * 128 : (side + 1) * 128]
            mine = (head_of == head) & (core == side)

            @pl.when(mine)
            def _(side=side):
                proj_in[head] = proj_out[row_y * 2 + side]

            @pl.when(jnp.logical_not(mine))
            def _(side=side):
                remote(
                    proj_out.at[row_y * 2 + side], proj_in.at[head], proj_sem.at[0], proj_sem.at[1],
                    device(zh, chip, side, head_of),
                ).start()

        return 0

    lax.fori_loop(0, 4, project, 0)

    def proj_wait(in_half, count):
        some, into = proj_out.at[pl.ds(0, count)], proj_in.at[pl.ds(0, count)]
        copy = remote(some, into, proj_sem.at[0], proj_sem.at[1], sibling)
        pl.when(in_half)(copy.wait_recv)
        return copy.wait_send

    in_half = core == head // 4
    left_seven = proj_wait(in_half, 7)
    left_eight = proj_wait(jnp.logical_not(in_half), 8)
    result = proj_in[0].astype(F32)
    for i in range(1, 8):
        result += proj_in[i].astype(F32)
    out_ref[...] = result[:, :cols].astype(BF16)

    sib_copy.wait_send()
    for copy in zh_copies:
        copy.wait_send()
    for rel in range(2):
        some = queries.at[rel, pl.ds(0, 15)]
        remote(some, some, q_send.at[rel], q_recv.at[rel, 0], sibling).wait_send()
    all_parts.wait_send()
    some = attended.at[pl.ds(0, 15)]
    remote(some, some, att_send.at[0], att_recv.at[0], sibling).wait_send()
    pl.when(in_half)(left_seven)
    pl.when(jnp.logical_not(in_half))(left_eight)


def shards(clean_query, noise, key_cache, value_cache, out_weight, row_run, limits, restored):
    shard_len, cols = key_cache.shape[0], out_weight.shape[1]
    vmem = pl.BlockSpec(memory_space=pltpu.VMEM)
    hbm = pl.BlockSpec(memory_space=pltpu.HBM)
    dma = pltpu.SemaphoreType.DMA
    return pl.pallas_call(
        kernel,
        out_shape=jax.ShapeDtypeStruct((64, cols), BF16),
        in_specs=[vmem, vmem, hbm, hbm, hbm, vmem, vmem, pl.BlockSpec(memory_space=pltpu.SMEM)],
        out_specs=vmem,
        scratch_shapes=[
            pltpu.VMEM((shard_len, HD), BF16),
            pltpu.VMEM((shard_len, HD), BF16),
            pltpu.VMEM((2, 16, 3 * HD), BF16),
            pltpu.VMEM((2, 16, 3 * HD), BF16),
            pltpu.VMEM((2, 16, BLOCK, HD), BF16),
            pltpu.VMEM((2 * HD, shard_len), BF16),
            pltpu.VMEM((shard_len, 2 * HD), BF16),
            pltpu.VMEM((CHUNK, 2 * HD), BF16),
            pltpu.VMEM((2, SUB, shard_len), F32),
            pltpu.VMEM((2, SUB, shard_len), BF16),
            pltpu.VMEM((2, SUB, 128), F32),
            pltpu.VMEM((32, PACK, HD), BF16),
            pltpu.VMEM((32, PACK, HD), BF16),
            pltpu.VMEM((PACK, HD), BF16),
            pltpu.VMEM((PACK, HD), BF16),
            pltpu.VMEM((16, BLOCK, HD), BF16),
            pltpu.VMEM((256, GROUP * HD), BF16),
            pltpu.VMEM((GROUP * HD, 256), BF16),
            pltpu.VMEM((8, 64, 128), BF16),
            pltpu.VMEM((8, 64, 128), BF16),
            pltpu.VMEM((512, 128), F32),
            pltpu.VMEM((32, 16, 128), F32),
            dma((3,)),
            dma((2,)),
            dma((2,)),
            dma((2,)),
            dma((2,)),
            dma((2,)),
            dma((2, 4)),
            dma((2,)),
            dma((2,)),
            dma((1,)),
            dma((4,)),
            dma((2,)),
        ],
        compiler_params=pltpu.CompilerParams(
            collective_id=0, has_side_effects=True, vmem_limit_bytes=60 << 20
        ),
        name="tracing",
    )(
        clean_query, noise, key_cache, value_cache, out_weight.T,
        row_run.reshape(4, 128), limits.reshape(4, 128), restored,
    )


def solution(mesh):
    placed = (
        P("seq", "head"),
        P("seq", "head"),
        P("seq", "head"),
        P("seq", "head"),
        P("head", "seq"),
        P(),
        P(),
        P(),
    )
    return jax.shard_map(
        shards, mesh=mesh, in_specs=placed, out_specs=P("head", "seq"), check_vma=False
    )
```

```python
import functools
import math

import jax
import jax.numpy as jnp
from jax import lax
from jax.experimental import pallas as pl
from jax.experimental.pallas import tpu as pltpu
from jax.sharding import PartitionSpec as P

MESH = pl.DeviceIdType.MESH
F32 = jnp.float32
BF16 = jnp.bfloat16

HD = 128
GROUP = 5
SCALE = math.log2(math.e) / math.sqrt(HD)
MASKED = -1e30
BLOCK = 16 * GROUP
PACK = BLOCK + 16
CHUNK = 4 * BLOCK
SUB = CHUNK // 2


def lanes_of(shape):
    return lax.broadcasted_iota(jnp.int32, shape, len(shape) - 1)


def pack_stat(rows):
    lane = lanes_of((16, 128))
    tile = jnp.zeros((16, 128), F32)
    for j, row in enumerate(rows):
        tile = jnp.where((lane % 8 == j) & (lane < 24), row, tile)
    high = tile.astype(BF16).astype(F32)
    rest = tile - high
    middle = rest.astype(BF16).astype(F32)
    low = rest - middle
    return jnp.where(lane < 8, high, jnp.where(lane < 16, middle, low)).astype(BF16)


def unpack_stat(tile):
    tile = tile.astype(F32)
    return tile + pltpu.roll(tile, 120, 1) + pltpu.roll(tile, 112, 1)


def head_column(tile, j):
    return jnp.broadcast_to(tile[:, j : j + 1], (16, 128))


def kernel(
    cq_ref, nz_ref, k_hbm, v_hbm, w_hbm, run_ref, lim_ref, restored_ref,
    out_ref,
    k_in, v_in, own_q, far_q, queries, rhs, v_ones, lhs, scores, probs, tops,
    partial, landed, zh_out, zh_in, attended, weights_t, weights, proj_out, proj_in, limit_col, share,
    load_sem, sib_sem, w_sem, zq_send, zq_recv, q_send, q_recv, part_sem, zh_sem, att_send, att_recv, proj_sem,
):
    seq, head = lax.axis_index("seq"), lax.axis_index("head")
    shard_len = k_hbm.shape[0]
    cols = w_hbm.shape[0]
    zh, chip, core = seq // 32, (seq // 2) % 16, seq % 2
    y, x = chip // 4, chip % 4

    def device(zh_, chip_, core_, head_):
        return (zh_ * 32 + chip_ * 2 + core_, head_)

    def plane_chip(i):
        return lax.rem(y + i // 4, 4) * 4 + lax.rem(x + i % 4, 4)

    sibling = device(zh, chip, 1 - core, head)
    zh_peer = device(1 - zh, chip, core, head)

    def remote(src, dst, send, recv, to):
        return pltpu.make_async_remote_copy(
            src_ref=src, dst_ref=dst, send_sem=send, recv_sem=recv, device_id=to, device_id_type=MESH
        )

    barrier = pltpu.get_barrier_semaphore()

    def greet(to):
        pl.semaphore_signal(barrier, inc=1, device_id=to, device_id_type=MESH)

    greet(zh_peer)
    greet(device(1 - zh, chip, 1 - core, head))

    for i in (4, 3, 5, 2, 6, 1, 7):
        greet(device(zh, chip, core, lax.rem(head + i, 8)))
    for i in range(15, 0, -1):
        greet(device(zh, plane_chip(i), core, head))
    greet(sibling)

    for side in range(2):
        pad = slice(side * 128 + cols, (side + 1) * 128)
        weights_t[pad, :] = jnp.zeros((128 - cols, weights_t.shape[1]), BF16)
    my_cols = weights_t.at[pl.ds(pl.multiple_of(core * 128, 128), cols), :]
    their_cols = weights_t.at[pl.ds(pl.multiple_of(128 - core * 128, 128), cols), :]
    loads = [
        pltpu.make_async_copy(src, dst, load_sem.at[i])
        for i, (src, dst) in enumerate(((k_hbm, k_in), (v_hbm, v_in), (w_hbm, my_cols)))
    ]
    for load in loads:
        load.start()

    limits = lim_ref[pl.ds(seq // 16, 1), :]
    runs = run_ref[pl.ds(seq // 16, 1), :]
    restored = jnp.zeros(runs.shape, jnp.int32)
    for r in range(restored_ref.shape[0]):
        restored = jnp.where(runs == r, restored_ref[r], restored)
    keep = jnp.where(limits - 1 == restored, 0.0, 1.0).astype(F32)
    mine = lax.broadcasted_iota(jnp.int32, (8, 128), 0) + (seq % 16) * 8 == lanes_of((8, 128))
    my_keep = jnp.sum(jnp.where(mine, jnp.broadcast_to(keep, (8, 128)), 0.0), axis=1, keepdims=True)
    half = 3 * HD
    mixed = cq_ref[...].astype(F32) + nz_ref[...].astype(F32) * my_keep
    rest = jnp.concatenate([mixed[:, half:], jnp.zeros((8, 2 * half - GROUP * HD), F32)], axis=1)
    own_q[core] = jnp.concatenate([mixed[:, :half], rest], axis=0).astype(BF16)

    loads[2].wait()

    pl.semaphore_wait(barrier, 25)

    zh_copies = [
        remote(own_q.at[core], far_q.at[core], zq_send.at[side], zq_recv.at[core], device(1 - zh, chip, side, head))
        for side in range(2)
    ]
    for copy in zh_copies:
        copy.start()
    sib_copy = remote(own_q.at[core], own_q.at[core], sib_sem.at[0], sib_sem.at[1], sibling)
    sib_copy.start()
    w_copy = remote(my_cols, my_cols, w_sem.at[0], w_sem.at[1], sibling)
    w_copy.start()

    def assemble(rel, pair):
        for j in range(GROUP):
            at = (slice(j // 3 * 8, j // 3 * 8 + 8), slice(j % 3 * HD, j % 3 * HD + HD))
            rows = jnp.concatenate([pair[k][at].astype(F32) for k in range(2)], axis=0)
            queries[rel, chip, j * 16 : (j + 1) * 16, :] = rows.astype(BF16)

    remote(own_q.at[1 - core], own_q.at[1 - core], sib_sem.at[0], sib_sem.at[1], sibling).wait_recv()
    assemble(0, [own_q[0], own_q[1]])

    def send_queries(rel):
        for i in range(1, 16):
            remote(
                queries.at[rel, chip], queries.at[rel, chip], q_send.at[rel], q_recv.at[rel, y],
                device(zh, plane_chip(i), core, head),
            ).start()

    send_queries(0)

    limits = lim_ref[...].astype(F32)
    diagonal = lax.broadcasted_iota(jnp.int32, (128, 128), 0) == lanes_of((128, 128))
    for t in range(limits.shape[0]):
        spread = jnp.where(diagonal, jnp.broadcast_to(limits[t : t + 1, :], (128, 128)), 0.0)
        limit_col[t * 128 : (t + 1) * 128, :] = jnp.broadcast_to(jnp.sum(spread, axis=1, keepdims=True), (128, 128))
    row = lax.broadcasted_iota(jnp.int32, (CHUNK, 128), 0)
    one_hot = ((row // BLOCK) * 16 + row % 16) == lanes_of((CHUNK, 128))
    lhs[:, HD:] = jnp.where(one_hot, 1.0, 0.0).astype(BF16)
    rhs[HD + 64 :, :] = jnp.zeros((64, shard_len), BF16)
    v_ones[:, HD:] = jnp.ones((shard_len, HD), BF16)
    loads[0].wait()
    rhs[:HD, :] = k_in[...].T
    loads[1].wait()
    v_ones[:, :HD] = v_in[...]
    w_copy.wait_send()
    remote(their_cols, their_cols, w_sem.at[0], w_sem.at[1], sibling).wait_recv()
    weights[...] = weights_t[...].T

    start = (seq * shard_len).astype(F32)

    def chunk(g, _):
        rel, t = g // 4, g % 4
        row_y = (y + t + t // 2 - 2 * (t // 3)) % 4
        zh_of = (zh + rel) % 2

        def arrive(count):
            some = queries.at[rel, pl.ds(0, count)]
            remote(some, some, q_send.at[rel], q_recv.at[rel, row_y], sibling).wait_recv()

        pl.when(t == 0)(lambda: arrive(3))
        pl.when(t != 0)(lambda: arrive(4))
        lhs[:, :HD] = queries[rel, pl.ds(row_y * 4, 4)].reshape(CHUNK, HD)
        first = pl.multiple_of(zh_of * 256 + row_y * 64, 64)
        limit = limit_col[pl.ds(first, 64), :] - start
        for at in range(0, shard_len, 128):
            position = (lanes_of((64, 128)) + at).astype(F32)
            rhs[HD : HD + 64, at : at + 128] = jnp.where(position < limit, 0.0, MASKED).astype(BF16)
        for i in range(4):
            if i < 2:
                scores[i] = jnp.dot(lhs[i * SUB : (i + 1) * SUB, :], rhs[...], preferred_element_type=F32)
            if 1 <= i < 3:
                part = scores[i - 1]
                top = jnp.max(part, axis=1, keepdims=True)
                tops[i - 1] = jnp.broadcast_to(top, (SUB, 128))
                probs[i - 1] = jnp.exp2((part - top) * SCALE).astype(BF16)
            if 2 <= i:
                both = jnp.dot(probs[i - 2], v_ones[...], preferred_element_type=F32)
                total = both[:, HD:]
                mean = (both[:, :HD] / total).astype(BF16)
                stat = tops[i - 2] * SCALE + jnp.log2(total)
                for b in range(2):
                    slot = row_y * 4 + (i - 2) * 2 + b
                    partial[rel * 16 + slot, :BLOCK, :] = mean[b * BLOCK : (b + 1) * BLOCK]
                    partial[rel * 16 + slot, BLOCK:, :] = pack_stat(
                        [stat[b * BLOCK + j * 16 : b * BLOCK + (j + 1) * 16] for j in range(GROUP)]
                    )

        def depart(i, _):
            owner = row_y * 4 + lax.rem(x + 2 + i, 4)
            mine = (owner == chip) & (zh_of == core)

            @pl.when(mine)
            def _():
                landed[seq % 32] = partial[rel * 16 + owner]

            @pl.when(jnp.logical_not(mine))
            def _():
                remote(
                    partial.at[rel * 16 + owner], landed.at[seq % 32], part_sem.at[0], part_sem.at[1],
                    device(zh, owner, zh_of, head),
                ).start()

            return 0

        lax.fori_loop(0, 4, depart, 0)
        return 0

    for side in range(2):
        remote(far_q.at[side], far_q.at[side], zq_send.at[side], zq_recv.at[side], sibling).wait_recv()
    assemble(1, [far_q[0], far_q[1]])
    send_queries(1)
    lax.fori_loop(0, 8, chunk, 0)

    all_parts = remote(partial.at[pl.ds(0, 31)], landed.at[pl.ds(0, 31)], part_sem.at[0], part_sem.at[1], sibling)
    all_parts.wait_recv()
    stats = [unpack_stat(landed[i, BLOCK:, :]) for i in range(32)]
    top = functools.reduce(jnp.maximum, stats)
    shares = [jnp.exp2(stat - top) for stat in stats]
    total = sum(shares[1:], shares[0])
    for i in range(32):
        share[i] = shares[i]

    def gather_mean(step, sums):
        for k in range(8):
            i = step * 8 + k
            weight = share[i]
            sums = tuple(
                sums[j] + head_column(weight, j) * landed[i, j * 16 : (j + 1) * 16, :].astype(F32)
                for j in range(GROUP)
            )
        return sums

    sums = lax.fori_loop(0, 4, gather_mean, (jnp.zeros((16, 128), F32),) * GROUP)
    stat = top + jnp.log2(total)
    means = [sums[j] / head_column(total, j) for j in range(GROUP)]
    for j in range(GROUP):
        zh_out[j * 16 : (j + 1) * 16, :] = means[j].astype(BF16)
    zh_out[BLOCK:, :] = pack_stat([head_column(stat, j) for j in range(GROUP)])
    zh_copy = remote(zh_out, zh_in, zh_sem.at[0], zh_sem.at[1], zh_peer)
    zh_copy.start()
    zh_copy.wait()
    other = unpack_stat(zh_in[BLOCK:, :])
    top = jnp.maximum(stat, other)
    here, there = jnp.exp2(stat - top), jnp.exp2(other - top)
    share_here, share_there = here / (here + there), there / (here + there)
    for j in range(GROUP):
        mixed = head_column(share_here, j) * means[j] + head_column(share_there, j) * zh_in[
            j * 16 : (j + 1) * 16, :
        ].astype(F32)
        attended[chip, j * 16 : (j + 1) * 16, :] = mixed.astype(BF16)

    for i in range(1, 16):
        remote(
            attended.at[chip], attended.at[chip], att_send.at[0], att_recv.at[y],
            device(zh, plane_chip(i), core, head),
        ).start()

    def project(t, _):
        row_y = (y + t + t // 2 - 2 * (t // 3)) % 4
        head_of = core * 4 + row_y

        def arrive(count):
            some = attended.at[pl.ds(0, count)]
            remote(some, some, att_send.at[0], att_recv.at[row_y], sibling).wait_recv()

        pl.when(t == 0)(lambda: arrive(3))
        pl.when(t != 0)(lambda: arrive(4))
        rows = jnp.concatenate(
            [attended[pl.ds(row_y * 4, 4), j * 16 : (j + 1) * 16, :].reshape(64, HD) for j in range(GROUP)], axis=1
        )
        both = jnp.dot(rows, weights[...], preferred_element_type=F32).astype(BF16)
        for side in range(2):
            proj_out[row_y * 2 + side] = both[:, side * 128 : (side + 1) * 128]
            mine = (head_of == head) & (core == side)

            @pl.when(mine)
            def _(side=side):
                proj_in[head] = proj_out[row_y * 2 + side]

            @pl.when(jnp.logical_not(mine))
            def _(side=side):
                remote(
                    proj_out.at[row_y * 2 + side], proj_in.at[head], proj_sem.at[0], proj_sem.at[1],
                    device(zh, chip, side, head_of),
                ).start()

        return 0

    lax.fori_loop(0, 4, project, 0)

    def proj_wait(in_half, count):
        some, into = proj_out.at[pl.ds(0, count)], proj_in.at[pl.ds(0, count)]
        copy = remote(some, into, proj_sem.at[0], proj_sem.at[1], sibling)
        pl.when(in_half)(copy.wait_recv)
        return copy.wait_send

    in_half = core == head // 4
    left_seven = proj_wait(in_half, 7)
    left_eight = proj_wait(jnp.logical_not(in_half), 8)
    result = proj_in[0].astype(F32)
    for i in range(1, 8):
        result += proj_in[i].astype(F32)
    out_ref[...] = result[:, :cols].astype(BF16)

    sib_copy.wait_send()
    for copy in zh_copies:
        copy.wait_send()
    for rel in range(2):
        some = queries.at[rel, pl.ds(0, 15)]
        remote(some, some, q_send.at[rel], q_recv.at[rel, 0], sibling).wait_send()
    all_parts.wait_send()
    some = attended.at[pl.ds(0, 15)]
    remote(some, some, att_send.at[0], att_recv.at[0], sibling).wait_send()
    pl.when(in_half)(left_seven)
    pl.when(jnp.logical_not(in_half))(left_eight)


def shards(clean_query, noise, key_cache, value_cache, out_weight, row_run, limits, restored):
    shard_len, cols = key_cache.shape[0], out_weight.shape[1]
    vmem = pl.BlockSpec(memory_space=pltpu.VMEM)
    hbm = pl.BlockSpec(memory_space=pltpu.HBM)
    dma = pltpu.SemaphoreType.DMA
    return pl.pallas_call(
        kernel,
        out_shape=jax.ShapeDtypeStruct((64, cols), BF16),
        in_specs=[vmem, vmem, hbm, hbm, hbm, vmem, vmem, pl.BlockSpec(memory_space=pltpu.SMEM)],
        out_specs=vmem,
        scratch_shapes=[
            pltpu.VMEM((shard_len, HD), BF16),
            pltpu.VMEM((shard_len, HD), BF16),
            pltpu.VMEM((2, 16, 3 * HD), BF16),
            pltpu.VMEM((2, 16, 3 * HD), BF16),
            pltpu.VMEM((2, 16, BLOCK, HD), BF16),
            pltpu.VMEM((2 * HD, shard_len), BF16),
            pltpu.VMEM((shard_len, 2 * HD), BF16),
            pltpu.VMEM((CHUNK, 2 * HD), BF16),
            pltpu.VMEM((2, SUB, shard_len), F32),
            pltpu.VMEM((2, SUB, shard_len), BF16),
            pltpu.VMEM((2, SUB, 128), F32),
            pltpu.VMEM((32, PACK, HD), BF16),
            pltpu.VMEM((32, PACK, HD), BF16),
            pltpu.VMEM((PACK, HD), BF16),
            pltpu.VMEM((PACK, HD), BF16),
            pltpu.VMEM((16, BLOCK, HD), BF16),
            pltpu.VMEM((256, GROUP * HD), BF16),
            pltpu.VMEM((GROUP * HD, 256), BF16),
            pltpu.VMEM((8, 64, 128), BF16),
            pltpu.VMEM((8, 64, 128), BF16),
            pltpu.VMEM((512, 128), F32),
            pltpu.VMEM((32, 16, 128), F32),
            dma((3,)),
            dma((2,)),
            dma((2,)),
            dma((2,)),
            dma((2,)),
            dma((2,)),
            dma((2, 4)),
            dma((2,)),
            dma((2,)),
            dma((1,)),
            dma((4,)),
            dma((2,)),
        ],
        compiler_params=pltpu.CompilerParams(
            collective_id=0, has_side_effects=True, vmem_limit_bytes=60 << 20
        ),
        name="tracing",
    )(
        clean_query, noise, key_cache, value_cache, out_weight.T,
        row_run.reshape(4, 128), limits.reshape(4, 128), restored,
    )


def solution(mesh):
    placed = (
        P("seq", "head"),
        P("seq", "head"),
        P("seq", "head"),
        P("seq", "head"),
        P("head", "seq"),
        P(),
        P(),
        P(),
    )
    return jax.shard_map(
        shards, mesh=mesh, in_specs=placed, out_specs=P("head", "seq"), check_vma=False
    )
```
